128 devices in a mesh: lat: 4 (over y_hi, core), lon: 32 (over y_lo, z, x).
Axes of the slice: x: 4, y: 4 (y_hi: 2, y_lo: 2; y = y_hi * 2 + y_lo), z: 4, core: 2. Of those that a mesh axis runs over, the one named last changes fastest.
Arguments:
- fields: bfloat16 [12, 96, 30720], P('lat', None, 'lon'), may hold values from -6 to 6
- surface_kind: int32 [96, 384], P('lat', 'lon'), may hold values from 0 to 2
- patch_weight: bfloat16 [80, 512], replicated, may hold values from -0.625 to 0.625
- level_embed: float32 [12, 512], replicated, may hold values from -6 to 6
- enc_gain: float32 [512], replicated, may hold values from 0.1 to 1.9
- latent_query: bfloat16 [3, 512], replicated, may hold values from -6 to 6
- kv_weight: bfloat16 [512, 1024], replicated, may hold values from -0.25 to 0.25
- enc_scale: float32 [8], replicated, may hold values from 0.5 to 100, as said below
- enc_out_weight: bfloat16 [512, 512], replicated, may hold values from -0.25 to 0.25
- kind_embed: float32 [3, 512], replicated, may hold values from -6 to 6
- attn_gain: float32 [512], replicated, may hold values from 0.1 to 1.9
- qkv_weight: bfloat16 [512, 1536], replicated, may hold values from -0.25 to 0.25
- swin_scale: float32 [8], replicated, may hold values from 0.5 to 100, as said below
- proj_weight: bfloat16 [512, 512], replicated, may hold values from -0.25 to 0.25
- mlp_gain: float32 [512], replicated, may hold values from 0.1 to 1.9
- mlp_up: bfloat16 [2048, 512], P(('lat', 'lon')), may hold values from -0.25 to 0.25
- mlp_down: bfloat16 [2048, 512], P(('lat', 'lon')), may hold values from -0.125 to 0.125
Outputs:
- latents_out: bfloat16 [3, 96, 384, 512], P(None, 'lat', 'lon')
The draws below stay inside these ranges and needn't reach their ends.
Inputs may be any that keep to these rules, and one draw needn't show every extreme that they name: `enc_scale`: one logit scale for each head. `swin_scale`: one logit scale for each head.
All inputs are finite; a program needn't handle non-finite values.
Results may differ from the reference program's by a relative error of at most 0.018.
The reference program's roundings to bfloat16 on the way count: a program that leaves them out, or rounds other values in their place, can miss the bound.
Values may be sent and summed in bfloat16 or wider, within the bound.
No kernel may reach another device: no remote copies, remote signals or barrier semaphores. Data moves between devices by JAX's collectives and lax.ppermute only.
A program may use at most 128 MiB of HBM per device.

```python
import math
import jax
import jax.numpy as jnp
from jax import lax

D = 512
HEADS = 8
FF = 2048
LEVELS = 12
LATENT = 3
KINDS = 3
WH = 6
WW = 12
CHAN = 80
PH = 96
PW = 384


def draw_enc_scale(key, part):
    key = jax.random.fold_in(key, 17)
    base_key = jax.random.fold_in(key, 0)
    scales = jnp.exp(jax.random.uniform(base_key, (HEADS,), jnp.float32, math.log(0.5), math.log(6.0)))
    return scales


def draw_swin_scale(key, part):
    key = jax.random.fold_in(key, 29)
    base_key = jax.random.fold_in(key, 0)
    scales = jnp.exp(jax.random.uniform(base_key, (HEADS,), jnp.float32, math.log(0.5), math.log(6.0)))
    return scales


def touch_ends(values, rng, least, largest):
    longest = values.shape.index(max(values.shape))
    spots = []
    for shift in (0, 1):
        where = [jax.random.randint(jax.random.fold_in(rng, axis), (), 0, length) for axis, length in enumerate(values.shape)]
        where[longest] = (where[longest] + shift) % values.shape[longest]
        spots.append(tuple(where))
    return values.at[spots[0]].set(least).at[spots[1]].set(largest)


def levels(rng, shape, shards, least, largest):
    gain = 1.0
    for axis_at, parts in shards:
        steps = jax.random.uniform(jax.random.fold_in(jax.random.fold_in(rng, 6), axis_at), (parts,), jnp.float32, least / len(shards), largest / len(shards))
        gain = gain * jnp.repeat(jnp.exp(steps), shape[axis_at] // parts).reshape((-1,) + (1,) * (len(shape) - 1 - axis_at))
    return gain


def scatter_about(key, dims, width, limit, shards=(), kind=jnp.bfloat16):
    level = levels(key, dims, shards, -0.22, 0.18) if shards else 1.0
    entries = jax.random.normal(key, dims, jnp.float32) * width * level
    return jnp.minimum(jnp.maximum(entries, -limit), limit).astype(kind)


def setup_inputs(seed: int = 0) -> dict:
    key_of = jax.random.split(jax.random.key(seed), 18)
    return {
        "fields": scatter_about(key_of[0], (LEVELS, PH, PW * CHAN), 1.0, 6.0, ((0, 4), (2, 32))),
        "surface_kind": touch_ends(jax.random.randint(key_of[1], (PH, PW), 0, KINDS), jax.random.fold_in(key_of[1], 1), 0, KINDS - 1).astype(jnp.int32),
        "patch_weight": scatter_about(key_of[2], (CHAN, D), CHAN ** -0.5, 0.625),
        "level_embed": scatter_about(key_of[3], (LEVELS, D), 1.0, 6.0, (), jnp.float32),
        "enc_gain": jnp.clip(1.0 + 0.18 * jax.random.normal(key_of[4], (D,), jnp.float32), 0.1, 1.9),
        "latent_query": scatter_about(key_of[5], (LATENT, D), 1.0, 6.0),
        "kv_weight": scatter_about(key_of[6], (D, 2 * D), D ** -0.5, 0.25),
        "enc_scale": draw_enc_scale(jax.random.fold_in(key_of[17], 71), 0),
        "enc_out_weight": scatter_about(key_of[8], (D, D), D ** -0.5, 0.25),
        "kind_embed": scatter_about(key_of[9], (KINDS, D), 1.0, 6.0, (), jnp.float32),
        "attn_gain": jnp.clip(1.0 + 0.18 * jax.random.normal(key_of[10], (D,), jnp.float32), 0.1, 1.9),
        "qkv_weight": scatter_about(key_of[11], (D, 3 * D), D ** -0.5, 0.25),
        "swin_scale": draw_swin_scale(jax.random.fold_in(key_of[17], 71), 0),
        "proj_weight": scatter_about(key_of[13], (D, D), D ** -0.5, 0.25),
        "mlp_gain": jnp.clip(1.0 + 0.18 * jax.random.normal(key_of[14], (D,), jnp.float32), 0.1, 1.9),
        "mlp_up": scatter_about(key_of[15], (FF, D), D ** -0.5, 0.25, ((0, 128),)),
        "mlp_down": scatter_about(key_of[16], (FF, D), FF ** -0.5, 0.125, ((0, 128),)),
    }


epsilon = 1e-05
masked_score = -1e+30

def layer_norm(values, gain_vector):
    average = lax.optimization_barrier(jnp.mean(values, axis=-1, keepdims=True))
    centred = values - average
    spread = lax.optimization_barrier(jnp.mean(centred * centred, axis=-1, keepdims=True))
    return centred * lax.rsqrt(spread + epsilon) * gain_vector

def encode_levels(patches, patch_weight, level_embed, enc_gain, latent_query, kv_weight, enc_scale, enc_out_weight):
    level_count, patch_count, channels = patches.shape
    model_width = patch_weight.shape[1]
    head_count = enc_scale.shape[0]
    head_size = model_width // head_count
    embedded = jnp.dot(patches.reshape(level_count * patch_count, channels), patch_weight, preferred_element_type=jnp.float32)
    embedded = embedded.reshape(level_count, patch_count, model_width) + level_embed[:, None, :]
    level_tokens = layer_norm(embedded, enc_gain).astype(jnp.bfloat16)
    keyval = jnp.dot(level_tokens.reshape(level_count * patch_count, model_width), kv_weight, preferred_element_type=jnp.float32).astype(jnp.bfloat16)
    keyval = keyval.reshape(level_count, patch_count, 2, head_count, head_size)
    queries = latent_query.reshape(-1, head_count, head_size)
    level_scores = jnp.einsum('lhd,kphd->klhp', queries.astype(jnp.float32), keyval[:, :, 0].astype(jnp.float32))
    level_scores = level_scores * (enc_scale / math.sqrt(head_size))[None, None, :, None]
    highest = lax.optimization_barrier(jnp.max(level_scores, axis=0, keepdims=True))
    raised = jnp.exp(level_scores - highest)
    level_weights = (raised / lax.optimization_barrier(jnp.sum(raised, axis=0, keepdims=True))).astype(jnp.bfloat16)
    pooled = jnp.einsum('klhp,kphd->plhd', level_weights.astype(jnp.float32), keyval[:, :, 1].astype(jnp.float32)).astype(jnp.bfloat16)
    latent_count = queries.shape[0]
    encoded = jnp.dot(pooled.reshape(patch_count * latent_count, model_width), enc_out_weight, preferred_element_type=jnp.float32)
    return encoded.reshape(patch_count, latent_count, model_width) + latent_query.astype(jnp.float32)[None]

def attend_windows(block_in, row_valid, attn_gain, qkv_weight, swin_scale):
    latent_count, row_count, col_count, model_width = block_in.shape
    head_count = swin_scale.shape[0]
    head_size = model_width // head_count
    row_windows = row_count // WH
    col_windows = col_count // WW
    window_size = latent_count * WH * WW
    normed = layer_norm(block_in.astype(jnp.float32), attn_gain).astype(jnp.bfloat16)
    projected = jnp.dot(normed.reshape(-1, model_width), qkv_weight, preferred_element_type=jnp.float32).astype(jnp.bfloat16)
    projected = projected.reshape(latent_count, row_windows, WH, col_windows, WW, 3, head_count, head_size)
    projected = projected.transpose(1, 3, 0, 2, 4, 5, 6, 7).reshape(row_windows * col_windows, window_size, 3, head_count, head_size)
    queries = projected[:, :, 0].astype(jnp.float32)
    key_part = projected[:, :, 1].astype(jnp.float32)
    value_part = projected[:, :, 2].astype(jnp.float32)
    window_scores = jnp.einsum('wqhd,wkhd->whqk', queries, key_part)
    window_scores = window_scores * (swin_scale / math.sqrt(head_size))[None, :, None, None]
    key_valid = jnp.broadcast_to(row_valid.reshape(1, row_windows, WH, 1, 1), (latent_count, row_windows, WH, col_windows, WW))
    key_valid = key_valid.transpose(1, 3, 0, 2, 4).reshape(row_windows * col_windows, 1, 1, window_size)
    window_scores = jnp.where(key_valid, window_scores, masked_score)
    highest = lax.optimization_barrier(jnp.max(window_scores, axis=-1, keepdims=True))
    raised = jnp.exp(window_scores - highest)
    window_weights = (raised / lax.optimization_barrier(jnp.sum(raised, axis=-1, keepdims=True))).astype(jnp.bfloat16)
    window_mixed = jnp.einsum('whqk,wkhd->wqhd', window_weights.astype(jnp.float32), value_part).astype(jnp.bfloat16)
    window_mixed = window_mixed.reshape(row_windows, col_windows, latent_count, WH, WW, model_width)
    return window_mixed.transpose(2, 0, 3, 1, 4, 5).reshape(latent_count, row_count, col_count, model_width)

def reference(fields, surface_kind, patch_weight, level_embed, enc_gain, latent_query, kv_weight, enc_scale, enc_out_weight, kind_embed, attn_gain, qkv_weight, swin_scale, proj_weight, mlp_gain, mlp_up, mlp_down):
    row_fields = fields.transpose(1, 0, 2)

    def encode_row(inputs):
        row_block, kind_row = inputs
        patches = row_block.reshape(LEVELS, PW, CHAN)
        encoded = encode_levels(patches, patch_weight, level_embed, enc_gain, latent_query, kv_weight, enc_scale, enc_out_weight)
        encoded = encoded + kind_embed[kind_row][:, None, :]
        return encoded.astype(jnp.bfloat16)
    latents = lax.map(encode_row, (row_fields, surface_kind)).transpose(2, 0, 1, 3)
    half_rows = WH // 2
    half_cols = WW // 2
    padded = jnp.pad(latents, ((0, 0), (half_rows, half_rows), (0, 0), (0, 0)))
    padded = jnp.roll(padded, half_cols, axis=2)
    row_windows = (PH + WH) // WH
    blocks = padded.reshape(LATENT, row_windows, WH, PW, D).transpose(1, 0, 2, 3, 4)

    def one_row(inputs):
        block_in, window_index = inputs
        global_row = window_index * WH - half_rows + jnp.arange(WH, dtype=jnp.int32)
        row_valid = (global_row >= 0) & (global_row < PH)
        window_mixed = attend_windows(block_in, row_valid, attn_gain, qkv_weight, swin_scale)
        projected = jnp.dot(window_mixed.reshape(-1, D), proj_weight, preferred_element_type=jnp.float32)
        return projected.astype(jnp.bfloat16).reshape(LATENT, WH, PW, D)
    attended = lax.map(one_row, (blocks, jnp.arange(row_windows, dtype=jnp.int32)))
    attended = attended.transpose(1, 0, 2, 3, 4).reshape(LATENT, PH + WH, PW, D)[:, half_rows:half_rows + PH]
    attended = jnp.roll(attended, -half_cols, axis=2)
    residual = latents.astype(jnp.float32) + attended.astype(jnp.float32)

    def mlp_row(residual_row):
        flat_rows = residual_row.reshape(-1, D)
        mlp_normed = layer_norm(flat_rows, mlp_gain).astype(jnp.bfloat16)
        hidden = jnp.dot(mlp_normed, mlp_up.T, preferred_element_type=jnp.float32)
        hidden = jax.nn.gelu(hidden, approximate=False).astype(jnp.bfloat16)
        output = flat_rows + jnp.dot(hidden, mlp_down, preferred_element_type=jnp.float32)
        return output.astype(jnp.bfloat16).reshape(residual_row.shape)
    return lax.map(mlp_row, residual.transpose(1, 0, 2, 3)).transpose(1, 0, 2, 3)
```

```python
import functools
import math

import jax
import jax.numpy as jnp
from jax import lax
from jax.experimental import pallas as pl
from jax.experimental.pallas import tpu as pltpu
from jax.sharding import PartitionSpec as P

WH = 6
WW = 12
HALF = WW // 2
SHIFT = WH // 2
LEVELS_EACH = 3
LATENT = 3
HEADS = 8
HEAD = 64
CHAN = 80
D = 512
ROWS = 24
SPAN = HALF * CHAN
WINDOWS = ROWS // WH
GROUP = WH * LATENT * HALF
PADDED = 112
STEP = LATENT * HALF
EDGE = 64

epsilon = 1e-05
masked_score = -1e30
f32 = jnp.float32
bf16 = jnp.bfloat16

VMEM = pl.BlockSpec(memory_space=pltpu.VMEM)
SMEM = pl.BlockSpec(memory_space=pltpu.SMEM)


def dot(a, b):
    return jnp.dot(a, b, preferred_element_type=f32)


def dot_nt(a, b):
    return lax.dot_general(a, b, (((1,), (1,)), ((), ())), preferred_element_type=f32)


def layer_norm(values, gain_vector):
    average = jnp.mean(values, axis=-1, keepdims=True)
    centred = values - average
    spread = jnp.mean(centred * centred, axis=-1, keepdims=True)
    return centred * lax.rsqrt(spread + epsilon) * gain_vector


def pack_kernel(place, fields, kind, *rest):
    outs, (left, right) = rest[:8], rest[8:]
    kinds = kind[...].astype(f32)
    kinds = jnp.concatenate([kinds[ROWS - SHIFT :], kinds[: ROWS - SHIFT]], axis=0)
    left[:, :, SPAN:] = jnp.zeros((4, 3 * ROWS, D - SPAN), f32)
    right[:, :, SPAN:] = jnp.zeros((4, 3 * ROWS, D - SPAN), f32)
    for level in range(LEVELS_EACH):
        part = fields[level].astype(f32)
        count = part.shape[0]
        part = jnp.concatenate([part[count - SHIFT :], part[: count - SHIFT]], axis=0)
        for to in range(4):
            rows = part[to * ROWS : (to + 1) * ROWS]
            left[to, level * ROWS : (level + 1) * ROWS, :SPAN] = rows[:, :SPAN]
            right[to, level * ROWS : (level + 1) * ROWS, :SPAN] = rows[:, SPAN:]
    for to in range(4):
        left[to, :ROWS, SPAN : SPAN + HALF] = kinds[:, :HALF]
        right[to, :ROWS, SPAN : SPAN + HALF] = kinds[:, HALF:]
    for step in range(4):
        to = lax.rem(place[0] + step, 4)
        outs[step][...] = left[to].astype(bf16)
        outs[4 + step][...] = right[to].astype(bf16)


def encode_kernel(
    place,
    enc_scale,
    piece0,
    piece1,
    piece2,
    piece3,
    patch_weight,
    level_embed,
    enc_gain,
    latent_query,
    kv_weight,
    enc_out_weight,
    kind_embed,
    out,
    shifted,
    spread,
    *,
    chunk,
):
    lat = place[0]
    pieces = [piece[...].astype(f32) for piece in (piece0, piece1, piece2, piece3)]
    row_at = lax.broadcasted_iota(jnp.int32, (ROWS, D - SPAN), 0)
    kinds = jnp.where(row_at < SHIFT, pieces[1][:ROWS, SPAN:], pieces[0][:ROWS, SPAN:])
    patches = jnp.concatenate(pieces, axis=0).astype(bf16)
    embeds = []
    for step in range(4):
        start = lax.rem(lat - step + 4, 4) * LEVELS_EACH
        for level in range(LEVELS_EACH):
            embeds.append(
                jnp.broadcast_to(level_embed[pl.ds(start + level, 1), :], (ROWS, D))
            )
    embeds = jnp.concatenate(embeds, axis=0)
    gain = enc_gain[...]
    shifted[...] = jnp.zeros(shifted.shape, bf16)
    for col in range(HALF):
        offset = col * CHAN % 128
        shifted[col, offset : offset + CHAN, :] = patch_weight[...]
    queries = latent_query[...].astype(f32)
    head_at = lax.broadcasted_iota(jnp.int32, (HEADS, D), 0)
    lane_at = lax.broadcasted_iota(jnp.int32, (HEADS, D), 1) // HEAD
    in_head = jnp.where(head_at == lane_at, 1.0, 0.0).astype(f32)
    query_rows = jnp.concatenate(
        [in_head * queries[latent : latent + 1] for latent in range(LATENT)], axis=0
    ).astype(bf16)
    nothing = jnp.zeros((HEADS, D), f32)
    widen = [
        jnp.concatenate(
            [in_head if at == latent else nothing for at in range(LATENT)], axis=0
        ).astype(bf16)
        for latent in range(LATENT)
    ]
    lane = lax.broadcasted_iota(jnp.int32, (1, LATENT * HEADS), 1) % HEADS
    scale = jnp.zeros((1, LATENT * HEADS), f32)
    for head in range(HEADS):
        scale = jnp.where(lane == head, enc_scale[head] / math.sqrt(HEAD), scale)
    count = patches.shape[0]
    levels = count // ROWS
    for first in range(0, HALF, chunk):
        tokens = []
        for col in range(first, first + chunk):
            base = col * CHAN // 128 * 128
            depth = min(192, D - base)
            embedded = dot(patches[:, base : base + depth], shifted[col, :depth, :]) + embeds
            tokens.append(layer_norm(embedded, gain).astype(bf16))
        tokens = jnp.concatenate(tokens, axis=0)
        keys = dot(tokens, kv_weight[:, :D]).astype(bf16)
        values = dot(tokens, kv_weight[:, D:]).astype(bf16).astype(f32)
        scores = dot_nt(keys, query_rows) * scale
        scores = scores.reshape(chunk, levels, ROWS, LATENT * HEADS)
        highest = jnp.max(scores, axis=1, keepdims=True)
        raised = jnp.exp(scores - highest)
        weights = raised / jnp.sum(raised, axis=1, keepdims=True)
        weights = weights.reshape(chunk * count, LATENT * HEADS).astype(bf16)
        pooled = []
        for latent in range(LATENT):
            wide = dot(weights, widen[latent]) * values
            pooled.append(jnp.sum(wide.reshape(chunk, levels, ROWS, D), axis=1))
        pooled = jnp.concatenate(
            [pooled[latent][at] for at in range(chunk) for latent in range(LATENT)], axis=0
        ).astype(bf16)
        encoded = dot(pooled, enc_out_weight[...])
        for at in range(chunk):
            col = first + at
            kind = kinds[:, col : col + 1]
            kind_add = jnp.where(
                kind < 0.5,
                kind_embed[0:1, :],
                jnp.where(kind < 1.5, kind_embed[1:2, :], kind_embed[2:3, :]),
            )
            for latent in range(LATENT):
                start = (at * LATENT + latent) * ROWS
                value = encoded[start : start + ROWS] + queries[latent : latent + 1] + kind_add
                value = value.astype(bf16).astype(f32)
                for tile in range(D // 128):
                    spread[tile, pl.ds(latent * HALF + col, ROWS, stride=STEP), :] = value[
                        :, tile * 128 : (tile + 1) * 128
                    ]
    for tile in range(D // 128):
        spread[tile, WINDOWS * GROUP :, :] = jnp.zeros((8, 128), f32)
        for window in range(WINDOWS):
            out[window * PADDED : (window + 1) * PADDED, tile * 128 : (tile + 1) * 128] = spread[
                tile, pl.ds(window * GROUP, PADDED), :
            ].astype(bf16)


def window_kernel(
    place,
    swin_scale,
    block0,
    block1,
    attn_gain,
    qkv_weight,
    proj_weight,
    resid0,
    resid1,
    qkv0,
    qkv1,
    mixed0,
    mixed1,
):
    gain = attn_gain[...]
    for block, qkv in ((block0, qkv0), (block1, qkv1)):
        normed = layer_norm(block[...].astype(f32), gain).astype(bf16)
        qkv[...] = dot(normed, qkv_weight[...]).astype(bf16)
    size = 2 * PADDED
    key_at = lax.broadcasted_iota(jnp.int32, (size, size), 1)
    key_at = jnp.where(key_at >= PADDED, key_at - PADDED, key_at)
    query_at = lax.broadcasted_iota(jnp.int32, (size, size), 0)
    query_at = jnp.where(query_at >= PADDED, query_at - PADDED, query_at)
    off = jnp.where(key_at < GROUP, 0.0, masked_score).astype(f32)
    apart = jnp.where((key_at < GROUP // 2) != (query_at < GROUP // 2), masked_score, 0.0)
    first_off = off + apart * jnp.where(place[0] == 0, 1.0, 0.0).astype(f32)
    off_row = off[0:1]
    lane = lax.broadcasted_iota(jnp.int32, (1, 128), 1)
    low = lane < HEAD
    sides = [jnp.where(low, 1.0, 0.0).astype(bf16), jnp.where(low, 0.0, 1.0).astype(bf16)]
    for window in range(WINDOWS):
        rows = slice(window * PADDED, (window + 1) * PADDED)
        bias = first_off if window == 0 else off_row
        for pair in range(HEADS // 2):
            query, key, value = [
                jnp.concatenate(
                    [
                        qkv[rows, part * D + pair * 128 : part * D + (pair + 1) * 128]
                        for qkv in (qkv0, qkv1)
                    ],
                    axis=0,
                )
                for part in range(3)
            ]
            sums = []
            for side in range(2):
                scores = dot_nt(query * sides[side], key) + bias
                highest = jnp.max(scores, axis=-1, keepdims=True)
                factor = swin_scale[2 * pair + side] * (math.log2(math.e) / math.sqrt(HEAD))
                raised = jnp.exp2((scores - highest) * factor)
                total = jnp.sum(raised, axis=-1, keepdims=True)
                weights = (raised * (1.0 / total)).astype(bf16)
                sums.append(dot(weights, value))
            both = jnp.where(low, sums[0], sums[1]).astype(bf16)
            mixed0[rows, pair * 128 : (pair + 1) * 128] = both[:PADDED]
            mixed1[rows, pair * 128 : (pair + 1) * 128] = both[PADDED:]
    for block, mixed, resid in ((block0, mixed0, resid0), (block1, mixed1, resid1)):
        attended = dot(mixed[...], proj_weight[...]).astype(bf16).astype(f32)
        resid[...] = block[...].astype(f32) + attended


def feed_kernel(resid, mlp_gain, mine, other, out, edge):
    values = resid[...]
    tokens = layer_norm(values, mlp_gain[...]).astype(bf16)
    total = values
    for weights in (mine, other):
        count = weights.shape[0]
        for start in range(0, count, 512):
            up = weights[start : start + 512, :D]
            down = weights[start : start + 512, D:]
            hidden = dot_nt(tokens, up)
            hidden = hidden * (1.0 + lax.erf(hidden * math.sqrt(0.5))) * 0.5
            total = total + dot(hidden.astype(bf16), down)
    total = total.astype(bf16)
    out[...] = total
    edge[...] = total[:EDGE]


def join_kernel(own, own_edge, far, far_edge, out, low, high):
    for source, tail, held in ((own, own_edge, low), (far, far_edge, high)):
        part = source[...].astype(f32)
        for window in range(WINDOWS):
            held[window * GROUP : (window + 1) * GROUP, :] = part[
                window * PADDED : window * PADDED + GROUP
            ]
        held[WINDOWS * GROUP : WINDOWS * GROUP + GROUP // 2, :] = tail[...].astype(f32)[
            : GROUP // 2
        ]
    for row in range(ROWS):
        for latent in range(LATENT):
            start = (row + SHIFT) * STEP + latent * HALF
            pair = jnp.concatenate(
                [low[start : start + HALF, :], high[start : start + HALF, :]], axis=0
            )
            out[latent, row] = pair.astype(bf16)


def params():
    return pltpu.CompilerParams(vmem_limit_bytes=56 * 1024 * 1024)


def struct(shape, dtype):
    return jax.ShapeDtypeStruct(shape, dtype)


def gather_weights(mlp_up, mlp_down, lon_count):
    held = jnp.concatenate([mlp_up, mlp_down], axis=1)
    for bits in (3, 12):
        unit = bits // 3
        moved = [
            lax.ppermute(
                held,
                "lon",
                [(i, (i & ~bits) | ((i + step * unit) & bits)) for i in range(lon_count)],
            )
            for step in (1, 2, 3)
        ]
        held = jnp.concatenate([held] + moved, axis=0)
    moved = [
        lax.ppermute(
            held,
            ("lat", "lon"),
            [
                (a * lon_count + b, ((a + 2 * far) % 4) * lon_count + (b ^ (16 * near)))
                for a in range(4)
                for b in range(lon_count)
            ],
        )
        for far, near in ((0, 1), (1, 0), (1, 1))
    ]
    mine = jnp.concatenate([held] + moved, axis=0)
    other = lax.ppermute(mine, "lat", [(a, a ^ 1) for a in range(4)])
    return mine, other


def move(array, lat_step, lon_step, lon_count):
    perm = [
        (a * lon_count + b, ((a + lat_step) % 4) * lon_count + (b + lon_step) % lon_count)
        for a in range(4)
        for b in range(lon_count)
    ]
    return lax.ppermute(array, ("lat", "lon"), perm)


def shards(
    lon_count,
    fields,
    surface_kind,
    patch_weight,
    level_embed,
    enc_gain,
    latent_query,
    kv_weight,
    enc_scale,
    enc_out_weight,
    kind_embed,
    attn_gain,
    qkv_weight,
    swin_scale,
    proj_weight,
    mlp_gain,
    mlp_up,
    mlp_down,
):
    place = lax.axis_index("lat").astype(jnp.int32).reshape(1)
    piece = struct((LEVELS_EACH * ROWS, D), bf16)
    packed = pl.pallas_call(
        pack_kernel,
        out_shape=[piece] * 8,
        in_specs=[SMEM, VMEM, VMEM],
        out_specs=[VMEM] * 8,
        scratch_shapes=[pltpu.VMEM((4, LEVELS_EACH * ROWS, D), f32)] * 2,
        compiler_params=params(),
        name="pack",
    )(place, fields, surface_kind)
    near = [packed[0]] + [move(packed[step], step, 0, lon_count) for step in (1, 2, 3)]
    far = [move(packed[4 + step], step, 1, lon_count) for step in range(4)]
    mine, other = gather_weights(mlp_up, mlp_down, lon_count)

    half_block = struct((WINDOWS * PADDED, D), bf16)
    encode = pl.pallas_call(
        functools.partial(encode_kernel, chunk=2),
        out_shape=half_block,
        in_specs=[SMEM, SMEM] + [VMEM] * 11,
        out_specs=VMEM,
        scratch_shapes=[
            pltpu.VMEM((HALF, 192, D), bf16),
            pltpu.VMEM((D // 128, WINDOWS * GROUP + 8, 128), f32),
        ],
        compiler_params=params(),
        name="encode",
    )

    def encoded(pieces):
        return encode(
            place,
            enc_scale,
            *pieces,
            patch_weight,
            level_embed,
            enc_gain.reshape(1, D),
            latent_query,
            kv_weight,
            enc_out_weight,
            kind_embed,
        )

    block1 = encoded(near)
    block0 = encoded(far)
    half_resid = struct((WINDOWS * PADDED, D), f32)
    resid0, resid1 = pl.pallas_call(
        window_kernel,
        out_shape=[half_resid] * 2,
        in_specs=[SMEM, SMEM] + [VMEM] * 5,
        out_specs=[VMEM] * 2,
        scratch_shapes=[pltpu.VMEM((WINDOWS * PADDED, 3 * D), bf16)] * 2
        + [pltpu.VMEM((WINDOWS * PADDED, D), bf16)] * 2,
        compiler_params=params(),
        name="window",
    )(place, swin_scale, block0, block1, attn_gain.reshape(1, D), qkv_weight, proj_weight)
    feed = pl.pallas_call(
        feed_kernel,
        out_shape=[half_block, struct((EDGE, D), bf16)],
        in_specs=[VMEM] * 4,
        out_specs=[VMEM] * 2,
        compiler_params=params(),
        name="feed",
    )
    gain = mlp_gain.reshape(1, D)
    out0, edge0 = feed(resid0, gain, mine, other)
    far_main = move(out0, 0, -1, lon_count)
    far_edge = move(edge0, -1, -1, lon_count)
    resid1, _ = lax.optimization_barrier((resid1, out0))
    out1, edge1 = feed(resid1, gain, mine, other)
    own_edge = move(edge1, -1, 0, lon_count)
    return pl.pallas_call(
        join_kernel,
        out_shape=struct((LATENT, ROWS, WW, D), bf16),
        in_specs=[VMEM] * 4,
        out_specs=VMEM,
        scratch_shapes=[pltpu.VMEM((WINDOWS * GROUP + 56, D), f32)] * 2,
        compiler_params=params(),
        name="join",
    )(out1, own_edge, far_main, far_edge)


def solution(mesh):
    return jax.shard_map(
        functools.partial(shards, mesh.shape["lon"]),
        mesh=mesh,
        in_specs=(
            P("lat", None, "lon"),
            P("lat", "lon"),
            P(),
            P(),
            P(),
            P(),
            P(),
            P(),
            P(),
            P(),
            P(),
            P(),
            P(),
            P(),
            P(),
            P(("lat", "lon"), None),
            P(("lat", "lon"), None),
        ),
        out_specs=P(None, "lat", "lon", None),
        check_vma=False,
    )
```

```python
import functools
import math

import jax
import jax.numpy as jnp
from jax import lax
from jax.experimental import pallas as pl
from jax.experimental.pallas import tpu as pltpu
from jax.sharding import PartitionSpec as P

WH = 6
WW = 12
HALF = WW // 2
SHIFT = WH // 2
LEVELS_EACH = 3
LATENT = 3
HEADS = 8
HEAD = 64
CHAN = 80
D = 512
ROWS = 24
SPAN = HALF * CHAN
WINDOWS = ROWS // WH
GROUP = WH * LATENT * HALF
PADDED = 112
STEP = LATENT * HALF
EDGE = 64
SKIP = 48

epsilon = 1e-05
masked_score = -1e30
f32 = jnp.float32
bf16 = jnp.bfloat16

VMEM = pl.BlockSpec(memory_space=pltpu.VMEM)
SMEM = pl.BlockSpec(memory_space=pltpu.SMEM)


def dot(a, b):
    return jnp.dot(a, b, preferred_element_type=f32)


def dot_nt(a, b):
    return lax.dot_general(a, b, (((1,), (1,)), ((), ())), preferred_element_type=f32)


def layer_norm(values, gain_vector):
    average = jnp.mean(values, axis=-1, keepdims=True)
    centred = values - average
    spread = jnp.mean(centred * centred, axis=-1, keepdims=True)
    return centred * lax.rsqrt(spread + epsilon) * gain_vector


def pack_kernel(place, fields, kind, mlp_up, mlp_down, *rest):
    outs, held, staged = rest[:4], rest[4], rest[5]
    held[:, :D] = mlp_up[...]
    held[:, D:] = mlp_down[...]
    row_at = lax.broadcasted_iota(jnp.int32, (ROWS, ROWS), 0)
    col_at = lax.broadcasted_iota(jnp.int32, (ROWS, ROWS), 1)
    one_hot = jnp.where(row_at == col_at, 1.0, 0.0).astype(bf16)
    kinds = dot_nt(one_hot, kind[...].astype(f32).astype(bf16))
    kinds = jnp.concatenate([kinds[ROWS - SHIFT :], kinds[: ROWS - SHIFT]], axis=0)
    nothing = jnp.zeros((4, 3 * ROWS, D - SPAN), f32)
    staged[:, :, SPAN:D] = nothing
    staged[:, :, D + SPAN :] = nothing
    for level in range(LEVELS_EACH):
        part = fields[level].astype(f32)
        count = part.shape[0]
        part = jnp.concatenate([part[count - SHIFT :], part[: count - SHIFT]], axis=0)
        for to in range(4):
            rows = part[to * ROWS : (to + 1) * ROWS]
            at = slice(level * ROWS, (level + 1) * ROWS)
            staged[to, at, :SPAN] = rows[:, :SPAN]
            staged[to, at, D : D + SPAN] = rows[:, SPAN:]
    for to in range(4):
        staged[to, :ROWS, SPAN : SPAN + HALF] = kinds[:, :HALF]
        staged[to, :ROWS, D + SPAN : D + SPAN + HALF] = kinds[:, HALF:]
    for step in range(4):
        to = lax.rem(place[0] + step, 4)
        outs[step][...] = staged[to].astype(bf16)


def encode_kernel(
    place,
    enc_scale,
    piece0,
    piece1,
    piece2,
    piece3,
    patch_weight,
    level_embed,
    enc_gain,
    latent_query,
    kv_weight,
    enc_out_weight,
    kind_embed,
    out,
    shifted,
    spread,
    *,
    chunk,
):
    lat = place[0]
    pieces = [piece[:, :D].astype(f32) for piece in (piece0, piece1, piece2, piece3)]
    row_at = lax.broadcasted_iota(jnp.int32, (ROWS, D - SPAN), 0)
    kinds = jnp.where(row_at < SHIFT, pieces[1][:ROWS, SPAN:], pieces[0][:ROWS, SPAN:])
    patches = jnp.concatenate(pieces, axis=0).astype(bf16)
    embeds = []
    for step in range(4):
        start = lax.rem(lat - step + 4, 4) * LEVELS_EACH
        for level in range(LEVELS_EACH):
            embeds.append(
                jnp.broadcast_to(level_embed[pl.ds(start + level, 1), :], (ROWS, D))
            )
    embeds = jnp.concatenate(embeds, axis=0)
    gain = enc_gain[...]
    shifted[...] = jnp.zeros(shifted.shape, bf16)
    for col in range(HALF):
        offset = col * CHAN % 128
        shifted[col, offset : offset + CHAN, :] = patch_weight[...]
    queries = latent_query[...].astype(f32)
    head_at = lax.broadcasted_iota(jnp.int32, (HEADS, D), 0)
    lane_at = lax.broadcasted_iota(jnp.int32, (HEADS, D), 1) // HEAD
    in_head = jnp.where(head_at == lane_at, 1.0, 0.0).astype(f32)
    query_rows = jnp.concatenate(
        [in_head * queries[latent : latent + 1] for latent in range(LATENT)], axis=0
    ).astype(bf16)
    nothing = jnp.zeros((HEADS, D), f32)
    widen = [
        jnp.concatenate(
            [in_head if at == latent else nothing for at in range(LATENT)], axis=0
        ).astype(bf16)
        for latent in range(LATENT)
    ]
    lane = lax.broadcasted_iota(jnp.int32, (1, LATENT * HEADS), 1) % HEADS
    scale = jnp.zeros((1, LATENT * HEADS), f32)
    for head in range(HEADS):
        scale = jnp.where(lane == head, enc_scale[head] / math.sqrt(HEAD), scale)
    count = patches.shape[0]
    levels = count // ROWS
    for first in range(0, HALF, chunk):
        tokens = []
        for col in range(first, first + chunk):
            base = col * CHAN // 128 * 128
            depth = min(192, D - base)
            embedded = dot(patches[:, base : base + depth], shifted[col, :depth, :]) + embeds
            tokens.append(layer_norm(embedded, gain).astype(bf16))
        tokens = jnp.concatenate(tokens, axis=0)
        keys = dot(tokens, kv_weight[:, :D]).astype(bf16)
        values = dot(tokens, kv_weight[:, D:]).astype(bf16).astype(f32)
        scores = dot_nt(keys, query_rows) * scale
        scores = scores.reshape(chunk, levels, ROWS, LATENT * HEADS)
        highest = jnp.max(scores, axis=1, keepdims=True)
        raised = jnp.exp(scores - highest)
        weights = raised / jnp.sum(raised, axis=1, keepdims=True)
        weights = weights.reshape(chunk * count, LATENT * HEADS).astype(bf16)
        pooled = []
        for latent in range(LATENT):
            wide = dot(weights, widen[latent]) * values
            pooled.append(jnp.sum(wide.reshape(chunk, levels, ROWS, D), axis=1))
        pooled = jnp.concatenate(
            [pooled[latent][at] for at in range(chunk) for latent in range(LATENT)], axis=0
        ).astype(bf16)
        encoded = dot(pooled, enc_out_weight[...])
        for at in range(chunk):
            col = first + at
            kind = kinds[:, col : col + 1]
            kind_add = jnp.where(
                kind < 0.5,
                kind_embed[0:1, :],
                jnp.where(kind < 1.5, kind_embed[1:2, :], kind_embed[2:3, :]),
            )
            for latent in range(LATENT):
                start = (at * LATENT + latent) * ROWS
                value = encoded[start : start + ROWS] + queries[latent : latent + 1] + kind_add
                value = value.astype(bf16).astype(f32)
                for tile in range(D // 128):
                    spread[tile, pl.ds(latent * HALF + col, ROWS, stride=STEP), :] = value[
                        :, tile * 128 : (tile + 1) * 128
                    ]
    for tile in range(D // 128):
        spread[tile, WINDOWS * GROUP :, :] = jnp.zeros((8, 128), f32)
        for window in range(WINDOWS):
            out[window * PADDED : (window + 1) * PADDED, tile * 128 : (tile + 1) * 128] = spread[
                tile, pl.ds(window * GROUP, PADDED), :
            ].astype(bf16)


def window_kernel(
    place,
    swin_scale,
    block0,
    block1,
    attn_gain,
    qkv_weight,
    proj_weight,
    resid0,
    resid1,
    qkv0,
    qkv1,
    mixed0,
    mixed1,
):
    gain = attn_gain[...]
    for block, qkv in ((block0, qkv0), (block1, qkv1)):
        normed = layer_norm(block[...].astype(f32), gain).astype(bf16)
        qkv[...] = dot(normed, qkv_weight[...]).astype(bf16)
    size = 2 * PADDED
    key_at = lax.broadcasted_iota(jnp.int32, (size, size), 1)
    key_at = jnp.where(key_at >= PADDED, key_at - PADDED, key_at)
    query_at = lax.broadcasted_iota(jnp.int32, (size, size), 0)
    query_at = jnp.where(query_at >= PADDED, query_at - PADDED, query_at)
    off = jnp.where(key_at < GROUP, 0.0, masked_score).astype(f32)
    apart = jnp.where((key_at < GROUP // 2) != (query_at < GROUP // 2), masked_score, 0.0)
    first_off = off + apart * jnp.where(place[0] == 0, 1.0, 0.0).astype(f32)
    off_row = off[0:1]
    lane = lax.broadcasted_iota(jnp.int32, (1, 128), 1)
    low = lane < HEAD
    sides = [jnp.where(low, 1.0, 0.0).astype(bf16), jnp.where(low, 0.0, 1.0).astype(bf16)]
    for window in range(WINDOWS):
        rows = slice(window * PADDED, (window + 1) * PADDED)
        bias = first_off if window == 0 else off_row
        for pair in range(HEADS // 2):
            query, key, value = [
                jnp.concatenate(
                    [
                        qkv[rows, part * D + pair * 128 : part * D + (pair + 1) * 128]
                        for qkv in (qkv0, qkv1)
                    ],
                    axis=0,
                )
                for part in range(3)
            ]
            sums = []
            for side in range(2):
                scores = dot_nt(query * sides[side], key) + bias
                highest = jnp.max(scores, axis=-1, keepdims=True)
                factor = swin_scale[2 * pair + side] * (math.log2(math.e) / math.sqrt(HEAD))
                raised = jnp.exp2((scores - highest) * factor)
                total = jnp.sum(raised, axis=-1, keepdims=True)
                weights = (raised * (1.0 / total)).astype(bf16)
                sums.append(dot(weights, value))
            both = jnp.where(low, sums[0], sums[1]).astype(bf16)
            mixed0[rows, pair * 128 : (pair + 1) * 128] = both[:PADDED]
            mixed1[rows, pair * 128 : (pair + 1) * 128] = both[PADDED:]
    for block, mixed, resid in ((block0, mixed0, resid0), (block1, mixed1, resid1)):
        attended = dot(mixed[...], proj_weight[...]).astype(bf16).astype(f32)
        resid[...] = block[...].astype(f32) + attended


def feed_rows(values, gain, mine, other):
    tokens = layer_norm(values, gain).astype(bf16)
    total = values
    for block in (mine, other):
        for start in range(0, block.shape[0], 512):
            up = block[start : start + 512, :D]
            down = block[start : start + 512, D:]
            hidden = dot_nt(tokens, up)
            hidden = hidden * (1.0 + lax.erf(hidden * math.sqrt(0.5))) * 0.5
            total = total + dot(hidden.astype(bf16), down)
    return total.astype(bf16)


def feed_far_kernel(far, near, mlp_gain, mine, other, out, far_edge, near_edge):
    values = jnp.concatenate([far[...], near[:EDGE]], axis=0)
    total = feed_rows(values, mlp_gain[...], mine, other)
    out[...] = total[: WINDOWS * PADDED]
    far_edge[...] = total[:EDGE]
    near_edge[...] = total[WINDOWS * PADDED :]


def feed_near_kernel(near, mlp_gain, mine, other, out):
    out[...] = feed_rows(near[SKIP:], mlp_gain[...], mine, other)


def join_kernel(own, own_edge, far, far_edge, out, held):
    for side, (source, tail, skip) in enumerate(((own, own_edge, SKIP), (far, far_edge, 0))):
        for tile in range(D // 128):
            lanes = slice(tile * 128, (tile + 1) * 128)
            for window in range(WINDOWS):
                first = skip if window == 0 else 0
                start = window * PADDED - skip + first
                rows = source[start : start + PADDED - first, lanes].astype(f32)
                held[side, tile, window * GROUP + first : (window + 1) * GROUP, :] = rows[
                    : GROUP - first
                ]
            held[side, tile, WINDOWS * GROUP :, :] = tail[:, lanes].astype(f32)[:56]
        for latent in range(LATENT):
            for col in range(HALF):
                start = SHIFT * STEP + latent * HALF + col
                for tile in range(D // 128):
                    out[
                        latent, side * HALF + col, :, tile * 128 : (tile + 1) * 128
                    ] = held[side, tile, pl.ds(start, ROWS, stride=STEP), :].astype(bf16)


def params():
    return pltpu.CompilerParams(vmem_limit_bytes=56 * 1024 * 1024)


def struct(shape, dtype):
    return jax.ShapeDtypeStruct(shape, dtype)


def after(array, *others):
    return lax.optimization_barrier((array, *others))[0]


def along(held, bits, lon_count):
    unit = bits // 3
    moved = [
        lax.ppermute(
            held,
            "lon",
            [(i, (i & ~bits) | ((i + step * unit) & bits)) for i in range(lon_count)],
        )
        for step in (1, 2, 3)
    ]
    return jnp.concatenate([held] + moved, axis=0)


def along_y(held, lon_count):
    moved = [
        lax.ppermute(
            held,
            ("lat", "lon"),
            [
                (a * lon_count + b, ((a + 2 * far) % 4) * lon_count + (b ^ (16 * near)))
                for a in range(4)
                for b in range(lon_count)
            ],
        )
        for far, near in ((0, 1), (1, 0), (1, 1))
    ]
    return jnp.concatenate([held] + moved, axis=0)


def move(array, lat_step, lon_step, lon_count):
    perm = [
        (a * lon_count + b, ((a + lat_step) % 4) * lon_count + (b + lon_step) % lon_count)
        for a in range(4)
        for b in range(lon_count)
    ]
    return lax.ppermute(array, ("lat", "lon"), perm)


def shards(
    lon_count,
    fields,
    surface_kind,
    patch_weight,
    level_embed,
    enc_gain,
    latent_query,
    kv_weight,
    enc_scale,
    enc_out_weight,
    kind_embed,
    attn_gain,
    qkv_weight,
    swin_scale,
    proj_weight,
    mlp_gain,
    mlp_up,
    mlp_down,
):
    place = lax.axis_index("lat").astype(jnp.int32).reshape(1)
    piece = struct((LEVELS_EACH * ROWS, 2 * D), bf16)
    *packed, held = pl.pallas_call(
        pack_kernel,
        out_shape=[piece] * 4 + [struct((mlp_up.shape[0], 2 * D), bf16)],
        in_specs=[SMEM] + [VMEM] * 4,
        out_specs=[VMEM] * 5,
        scratch_shapes=[pltpu.VMEM((4, LEVELS_EACH * ROWS, 2 * D), f32)],
        compiler_params=params(),
        name="pack",
    )(place, fields, surface_kind.T, mlp_up, mlp_down)
    held = along(held, 3, lon_count)
    near = [packed[0]] + [move(packed[step], step, 0, lon_count) for step in (1, 2, 3)]
    held = along(held, 12, lon_count)
    far = move(jnp.concatenate([piece[:, D:] for piece in near], axis=0), 0, 1, lon_count)

    half_block = struct((WINDOWS * PADDED, D), bf16)
    encode = pl.pallas_call(
        functools.partial(encode_kernel, chunk=2),
        out_shape=half_block,
        in_specs=[SMEM, SMEM] + [VMEM] * 11,
        out_specs=VMEM,
        scratch_shapes=[
            pltpu.VMEM((HALF, 192, D), bf16),
            pltpu.VMEM((D // 128, WINDOWS * GROUP + 8, 128), f32),
        ],
        compiler_params=params(),
        name="encode",
    )

    def encoded(pieces):
        return encode(
            place,
            enc_scale,
            *pieces,
            patch_weight,
            level_embed,
            enc_gain.reshape(1, D),
            latent_query,
            kv_weight,
            enc_out_weight,
            kind_embed,
        )

    block1 = encoded(near)
    mine = along_y(after(held, block1), lon_count)
    rows = LEVELS_EACH * ROWS
    block0 = encoded([far[step * rows : (step + 1) * rows] for step in range(4)])
    half_resid = struct((WINDOWS * PADDED, D), f32)
    resid0, resid1 = pl.pallas_call(
        window_kernel,
        out_shape=[half_resid] * 2,
        in_specs=[SMEM, SMEM] + [VMEM] * 5,
        out_specs=[VMEM] * 2,
        scratch_shapes=[pltpu.VMEM((WINDOWS * PADDED, 3 * D), bf16)] * 2
        + [pltpu.VMEM((WINDOWS * PADDED, D), bf16)] * 2,
        compiler_params=params(),
        name="window",
    )(place, swin_scale, block0, block1, attn_gain.reshape(1, D), qkv_weight, proj_weight)
    mine = after(mine, resid0)
    other = lax.ppermute(mine, "lat", [(a, a ^ 1) for a in range(4)])
    gain = mlp_gain.reshape(1, D)
    edge = struct((EDGE, D), bf16)
    out0, edge0, edge1 = pl.pallas_call(
        feed_far_kernel,
        out_shape=[half_block, edge, edge],
        in_specs=[VMEM] * 5,
        out_specs=[VMEM] * 3,
        compiler_params=params(),
        name="feed_far",
    )(resid0, resid1, gain, mine, other)
    far_main = move(out0, 0, -1, lon_count)
    far_edge = move(edge0, -1, -1, lon_count)
    own_edge = move(edge1, -1, 0, lon_count)
    out1 = pl.pallas_call(
        feed_near_kernel,
        out_shape=struct((WINDOWS * PADDED - SKIP, D), bf16),
        in_specs=[VMEM] * 4,
        out_specs=VMEM,
        compiler_params=params(),
        name="feed_near",
    )(after(resid1, out0), gain, mine, other)
    joined = pl.pallas_call(
        join_kernel,
        out_shape=struct((LATENT, WW, ROWS, D), bf16),
        in_specs=[VMEM] * 4,
        out_specs=VMEM,
        scratch_shapes=[pltpu.VMEM((2, D // 128, WINDOWS * GROUP + 56, 128), f32)],
        compiler_params=params(),
        name="join",
    )(out1, own_edge, far_main, far_edge)
    return joined.transpose(0, 2, 1, 3)


def solution(mesh):
    return jax.shard_map(
        functools.partial(shards, mesh.shape["lon"]),
        mesh=mesh,
        in_specs=(
            P("lat", None, "lon"),
            P("lat", "lon"),
            P(),
            P(),
            P(),
            P(),
            P(),
            P(),
            P(),
            P(),
            P(),
            P(),
            P(),
            P(),
            P(),
            P(("lat", "lon"), None),
            P(("lat", "lon"), None),
        ),
        out_specs=P(None, "lat", "lon", None),
        check_vma=False,
    )
```

```python
import functools
import math

import jax
import jax.numpy as jnp
from jax import lax
from jax.experimental import pallas as pl
from jax.experimental.pallas import tpu as pltpu
from jax.sharding import PartitionSpec as P

WH = 6
WW = 12
HALF = WW // 2
SHIFT = WH // 2
LEVELS_EACH = 3
LATENT = 3
HEADS = 8
HEAD = 64
CHAN = 80
D = 512
ROWS = 24
SPAN = HALF * CHAN
WINDOWS = ROWS // WH
GROUP = WH * LATENT * HALF
PADDED = 112
STEP = LATENT * HALF
EDGE = 64
SKIP = 48
GAIN = 12
QUERY = 13
KIND = 16
ATTN = 19
MLP = 20

epsilon = 1e-05
masked_score = -1e30
f32 = jnp.float32
bf16 = jnp.bfloat16

VMEM = pl.BlockSpec(memory_space=pltpu.VMEM)
ANY = pl.BlockSpec(memory_space=pl.ANY)
SMEM = pl.BlockSpec(memory_space=pltpu.SMEM)


def dot(a, b):
    return jnp.dot(a, b, preferred_element_type=f32)


def dot_nt(a, b):
    return lax.dot_general(a, b, (((1,), (1,)), ((), ())), preferred_element_type=f32)


def layer_norm(values, gain_vector):
    average = jnp.mean(values, axis=-1, keepdims=True)
    centred = values - average
    spread = jnp.mean(centred * centred, axis=-1, keepdims=True)
    return centred * lax.rsqrt(spread + epsilon) * gain_vector


def pack_kernel(place, fields, kind, mlp_up, mlp_down, *rest):
    outs, held, staged = rest[:4], rest[4], rest[5]
    held[:, :D] = mlp_up[...]
    held[:, D:] = mlp_down[...]
    row_at = lax.broadcasted_iota(jnp.int32, (ROWS, ROWS), 0)
    col_at = lax.broadcasted_iota(jnp.int32, (ROWS, ROWS), 1)
    one_hot = jnp.where(row_at == col_at, 1.0, 0.0).astype(bf16)
    kinds = dot_nt(one_hot, kind[...].astype(f32).astype(bf16))
    kinds = jnp.concatenate([kinds[ROWS - SHIFT :], kinds[: ROWS - SHIFT]], axis=0)
    nothing = jnp.zeros((4, 3 * ROWS, D - SPAN), f32)
    staged[:, :, SPAN:D] = nothing
    staged[:, :, D + SPAN :] = nothing
    for level in range(LEVELS_EACH):
        part = fields[level].astype(f32)
        count = part.shape[0]
        part = jnp.concatenate([part[count - SHIFT :], part[: count - SHIFT]], axis=0)
        for to in range(4):
            rows = part[to * ROWS : (to + 1) * ROWS]
            at = slice(level * ROWS, (level + 1) * ROWS)
            staged[to, at, :SPAN] = rows[:, :SPAN]
            staged[to, at, D : D + SPAN] = rows[:, SPAN:]
    for to in range(4):
        staged[to, :ROWS, SPAN : SPAN + HALF] = kinds[:, :HALF]
        staged[to, :ROWS, D + SPAN : D + SPAN + HALF] = kinds[:, HALF:]
    for step in range(4):
        to = lax.rem(place[0] + step, 4)
        outs[step][...] = staged[to].astype(bf16)


def prepare_kernel(
    level_embed,
    enc_gain,
    latent_query,
    kind_embed,
    attn_gain,
    mlp_gain,
    patch_weight,
    *rest,
):
    fars, small, shifted, nears, sems = rest[:4], rest[4], rest[5], rest[6:10], rest[10]
    copies = [
        pltpu.make_async_copy(far, near, sems.at[at])
        for at, (far, near) in enumerate(zip(fars, nears))
    ]
    for copy in copies:
        copy.start()
    small[...] = jnp.concatenate(
        [
            level_embed[...],
            enc_gain[...],
            latent_query[...].astype(f32),
            kind_embed[...],
            attn_gain[...],
            mlp_gain[...],
            jnp.zeros((3, D), f32),
        ],
        axis=0,
    )
    shifted[...] = jnp.zeros(shifted.shape, bf16)
    for col in range(HALF):
        offset = col * CHAN % 128
        shifted[col, offset : offset + CHAN, :] = patch_weight[...]
    for copy in copies:
        copy.wait()


def encode_kernel(
    place,
    enc_scale,
    piece0,
    piece1,
    piece2,
    piece3,
    small,
    shifted,
    kv_weight,
    enc_out_weight,
    out,
    spread,
    *,
    side,
    chunk,
):
    lat = place[0]
    lanes = slice(side * D, (side + 1) * D)
    pieces = [piece[:, lanes].astype(f32) for piece in (piece0, piece1, piece2, piece3)]
    row_at = lax.broadcasted_iota(jnp.int32, (ROWS, D - SPAN), 0)
    kinds = jnp.where(row_at < SHIFT, pieces[1][:ROWS, SPAN:], pieces[0][:ROWS, SPAN:])
    patches = jnp.concatenate(pieces, axis=0).astype(bf16)
    embeds = []
    for step in range(4):
        start = lax.rem(lat - step + 4, 4) * LEVELS_EACH
        for level in range(LEVELS_EACH):
            embeds.append(
                jnp.broadcast_to(small[pl.ds(start + level, 1), :], (ROWS, D))
            )
    embeds = jnp.concatenate(embeds, axis=0)
    gain = small[GAIN : GAIN + 1]
    queries = small[QUERY : QUERY + LATENT]
    kind_embed = small[KIND : KIND + 3]
    head_at = lax.broadcasted_iota(jnp.int32, (HEADS, D), 0)
    lane_at = lax.broadcasted_iota(jnp.int32, (HEADS, D), 1) // HEAD
    in_head = jnp.where(head_at == lane_at, 1.0, 0.0).astype(f32)
    query_rows = jnp.concatenate(
        [in_head * queries[latent : latent + 1] for latent in range(LATENT)], axis=0
    ).astype(bf16)
    nothing = jnp.zeros((HEADS, D), f32)
    widen = [
        jnp.concatenate(
            [in_head if at == latent else nothing for at in range(LATENT)], axis=0
        ).astype(bf16)
        for latent in range(LATENT)
    ]
    lane = lax.broadcasted_iota(jnp.int32, (1, LATENT * HEADS), 1) % HEADS
    scale = jnp.zeros((1, LATENT * HEADS), f32)
    for head in range(HEADS):
        scale = jnp.where(lane == head, enc_scale[head] / math.sqrt(HEAD), scale)
    count = patches.shape[0]
    levels = count // ROWS
    for first in range(0, HALF, chunk):
        tokens = []
        for col in range(first, first + chunk):
            base = col * CHAN // 128 * 128
            depth = min(192, D - base)
            embedded = dot(patches[:, base : base + depth], shifted[col, :depth, :]) + embeds
            tokens.append(layer_norm(embedded, gain).astype(bf16))
        tokens = jnp.concatenate(tokens, axis=0)
        keys = dot(tokens, kv_weight[:, :D]).astype(bf16)
        values = dot(tokens, kv_weight[:, D:]).astype(bf16).astype(f32)
        scores = dot_nt(keys, query_rows) * scale
        scores = scores.reshape(chunk, levels, ROWS, LATENT * HEADS)
        highest = jnp.max(scores, axis=1, keepdims=True)
        raised = jnp.exp(scores - highest)
        weights = raised / jnp.sum(raised, axis=1, keepdims=True)
        weights = weights.reshape(chunk * count, LATENT * HEADS).astype(bf16)
        pooled = []
        for latent in range(LATENT):
            wide = dot(weights, widen[latent]) * values
            pooled.append(jnp.sum(wide.reshape(chunk, levels, ROWS, D), axis=1))
        pooled = jnp.concatenate(
            [pooled[latent][at] for at in range(chunk) for latent in range(LATENT)], axis=0
        ).astype(bf16)
        encoded = dot(pooled, enc_out_weight[...])
        for at in range(chunk):
            col = first + at
            kind = kinds[:, col : col + 1]
            kind_add = jnp.where(
                kind < 0.5,
                kind_embed[0:1],
                jnp.where(kind < 1.5, kind_embed[1:2], kind_embed[2:3]),
            )
            for latent in range(LATENT):
                start = (at * LATENT + latent) * ROWS
                value = encoded[start : start + ROWS] + queries[latent : latent + 1] + kind_add
                value = value.astype(bf16).astype(f32)
                for tile in range(D // 128):
                    spread[tile, pl.ds(latent * HALF + col, ROWS, stride=STEP), :] = value[
                        :, tile * 128 : (tile + 1) * 128
                    ]
    for tile in range(D // 128):
        spread[tile, WINDOWS * GROUP :, :] = jnp.zeros((8, 128), f32)
        for window in range(WINDOWS):
            out[window * PADDED : (window + 1) * PADDED, tile * 128 : (tile + 1) * 128] = spread[
                tile, pl.ds(window * GROUP, PADDED), :
            ].astype(bf16)


def window_kernel(
    place,
    swin_scale,
    own,
    halo,
    small,
    qkv_weight,
    proj_weight,
    resid,
    own_qkv,
    halo_kv,
    mixed,
):
    gain = small[ATTN : ATTN + 1]
    normed = layer_norm(own[...].astype(f32), gain).astype(bf16)
    own_qkv[...] = dot(normed, qkv_weight[...]).astype(bf16)
    normed = layer_norm(halo[...].astype(f32), gain).astype(bf16)
    halo_kv[...] = dot(normed, qkv_weight[:, D:]).astype(bf16)
    size = 2 * PADDED
    key_at = lax.broadcasted_iota(jnp.int32, (size, size), 1)
    key_at = jnp.where(key_at >= PADDED, key_at - PADDED, key_at)
    query_at = lax.broadcasted_iota(jnp.int32, (size, size), 0)
    query_at = jnp.where(query_at >= PADDED, query_at - PADDED, query_at)
    off = jnp.where(key_at < GROUP, 0.0, masked_score).astype(f32)
    apart = jnp.where((key_at < GROUP // 2) != (query_at < GROUP // 2), masked_score, 0.0)
    first_off = off + apart * jnp.where(place[0] == 0, 1.0, 0.0).astype(f32)
    off_row = off[0:1]
    lane = lax.broadcasted_iota(jnp.int32, (1, 128), 1)
    low = lane < HEAD
    sides = [jnp.where(low, 1.0, 0.0).astype(bf16), jnp.where(low, 0.0, 1.0).astype(bf16)]
    first_side = lax.broadcasted_iota(jnp.int32, (size, 1), 0) < PADDED
    unit = math.log2(math.e) / math.sqrt(HEAD)
    factors = [
        jnp.where(first_side, swin_scale[2 * pair] * unit, swin_scale[2 * pair + 1] * unit)
        for pair in range(HEADS // 2)
    ]
    for window in range(WINDOWS):
        rows = slice(window * PADDED, (window + 1) * PADDED)
        bias = first_off if window == 0 else off_row
        for pair in range(HEADS // 2):
            lanes = [slice(part * D + pair * 128, part * D + pair * 128 + 128) for part in range(3)]
            query = own_qkv[rows, lanes[0]]
            key = jnp.concatenate([own_qkv[rows, lanes[1]], halo_kv[rows, lanes[0]]], axis=0)
            value = jnp.concatenate([own_qkv[rows, lanes[2]], halo_kv[rows, lanes[1]]], axis=0)
            both = jnp.concatenate([query * sides[0], query * sides[1]], axis=0)
            scores = dot_nt(both, key) + bias
            highest = jnp.max(scores, axis=-1, keepdims=True)
            raised = jnp.exp2((scores - highest) * factors[pair])
            total = jnp.sum(raised, axis=-1, keepdims=True)
            weights = (raised * (1.0 / total)).astype(bf16)
            sums = dot(weights, value)
            mixed[rows, lanes[0]] = jnp.where(low, sums[:PADDED], sums[PADDED:]).astype(bf16)
    attended = dot(mixed[...], proj_weight[...]).astype(bf16).astype(f32)
    resid[...] = own[...].astype(f32) + attended


def feed_rows(values, gain, mine, other):
    tokens = layer_norm(values, gain).astype(bf16)
    total = values
    for block in (mine, other):
        for start in range(0, block.shape[0], 512):
            up = block[start : start + 512, :D]
            down = block[start : start + 512, D:]
            hidden = dot_nt(tokens, up)
            hidden = hidden * (1.0 + lax.erf(hidden * math.sqrt(0.5))) * 0.5
            total = total + dot(hidden.astype(bf16), down)
    return total.astype(bf16)


def feed_first_kernel(left, right, small, mine, other, out, edges):
    values = jnp.concatenate([left[...], right[:EDGE]], axis=0)
    total = feed_rows(values, small[MLP : MLP + 1], mine, other)
    out[...] = total[: WINDOWS * PADDED]
    edges[:EDGE] = total[:EDGE]
    edges[EDGE:] = total[WINDOWS * PADDED :]


def feed_rest_kernel(right, small, mine, other, out):
    out[...] = feed_rows(right[SKIP:], small[MLP : MLP + 1], mine, other)


def join_kernel(left, right, edges, out, held):
    for side, (source, skip) in enumerate(((left, 0), (right, SKIP))):
        for tile in range(D // 128):
            lanes = slice(tile * 128, (tile + 1) * 128)
            for window in range(WINDOWS):
                first = skip if window == 0 else 0
                start = window * PADDED - skip + first
                rows = source[start : start + PADDED - first, lanes].astype(f32)
                held[side, tile, window * GROUP + first : (window + 1) * GROUP, :] = rows[
                    : GROUP - first
                ]
            tail = edges[side * EDGE : (side + 1) * EDGE, lanes].astype(f32)
            held[side, tile, WINDOWS * GROUP :, :] = tail[:56]
        for latent in range(LATENT):
            for col in range(HALF):
                start = SHIFT * STEP + latent * HALF + col
                for tile in range(D // 128):
                    out[
                        latent, side * HALF + col, :, tile * 128 : (tile + 1) * 128
                    ] = held[side, tile, pl.ds(start, ROWS, stride=STEP), :].astype(bf16)


def params():
    return pltpu.CompilerParams(vmem_limit_bytes=32 * 1024 * 1024)


def struct(shape, dtype):
    return jax.ShapeDtypeStruct(shape, dtype)


def after(array, *others):
    return lax.optimization_barrier((array, *others))[0]


def along(held, bits, lon_count):
    unit = bits // 3
    moved = [
        lax.ppermute(
            held,
            "lon",
            [(i, (i & ~bits) | ((i + step * unit) & bits)) for i in range(lon_count)],
        )
        for step in (1, 2, 3)
    ]
    return jnp.concatenate([held] + moved, axis=0)


def along_y(held, lon_count):
    moved = [
        lax.ppermute(
            held,
            ("lat", "lon"),
            [
                (a * lon_count + b, ((a + 2 * far) % 4) * lon_count + (b ^ (16 * near)))
                for a in range(4)
                for b in range(lon_count)
            ],
        )
        for far, near in ((0, 1), (1, 0), (1, 1))
    ]
    return [held] + moved


def near_by(array):
    return pltpu.with_memory_space_constraint(array, pltpu.VMEM)


def far_off(array):
    return pltpu.with_memory_space_constraint(array, pltpu.HBM)


def move(array, lat_step, lon_step, lon_count):
    perm = [
        (a * lon_count + b, ((a + lat_step) % 4) * lon_count + (b + lon_step) % lon_count)
        for a in range(4)
        for b in range(lon_count)
    ]
    return lax.ppermute(array, ("lat", "lon"), perm)


def shards(
    lon_count,
    fields,
    surface_kind,
    patch_weight,
    level_embed,
    enc_gain,
    latent_query,
    kv_weight,
    enc_scale,
    enc_out_weight,
    kind_embed,
    attn_gain,
    qkv_weight,
    swin_scale,
    proj_weight,
    mlp_gain,
    mlp_up,
    mlp_down,
):
    place = lax.axis_index("lat").astype(jnp.int32).reshape(1)
    piece = struct((LEVELS_EACH * ROWS, 2 * D), bf16)
    *packed, held = pl.pallas_call(
        pack_kernel,
        out_shape=[piece] * 4 + [struct((mlp_up.shape[0], 2 * D), bf16)],
        in_specs=[SMEM] + [VMEM] * 4,
        out_specs=[VMEM] * 5,
        scratch_shapes=[pltpu.VMEM((4, LEVELS_EACH * ROWS, 2 * D), f32)],
        compiler_params=params(),
        name="pack",
    )(
        place,
        far_off(fields),
        far_off(surface_kind.T),
        far_off(mlp_up),
        far_off(mlp_down),
    )
    held = along(held, 3, lon_count)
    near = [packed[0]] + [move(packed[step], step, 0, lon_count) for step in (1, 2, 3)]
    held = along(held, 12, lon_count)
    half_block = struct((WINDOWS * PADDED, D), bf16)
    half_resid = struct((WINDOWS * PADDED, D), f32)

    weights = (kv_weight, enc_out_weight, qkv_weight, proj_weight)
    small, shifted, kv_near, out_near, qkv_near, proj_near = [
        near_by(array)
        for array in pl.pallas_call(
            prepare_kernel,
            out_shape=[pltpu.VMEM((24, D), f32), pltpu.VMEM((HALF, 192, D), bf16)]
            + [pltpu.VMEM(weight.shape, bf16) for weight in weights],
            in_specs=[VMEM] * 7 + [ANY] * 4,
            out_specs=[VMEM] * 6,
            scratch_shapes=[pltpu.SemaphoreType.DMA((4,))],
            compiler_params=params(),
            name="prepare",
        )(
            far_off(after(level_embed, *packed)),
            far_off(enc_gain.reshape(1, D)),
            far_off(latent_query),
            far_off(kind_embed),
            far_off(attn_gain.reshape(1, D)),
            far_off(mlp_gain.reshape(1, D)),
            far_off(patch_weight),
            *[far_off(weight) for weight in weights],
        )
    ]

    def encode(side, pieces):
        return pl.pallas_call(
            functools.partial(encode_kernel, side=side, chunk=6),
            out_shape=half_block,
            in_specs=[SMEM, SMEM] + [VMEM] * 8,
            out_specs=VMEM,
            scratch_shapes=[pltpu.VMEM((D // 128, WINDOWS * GROUP + 8, 128), f32)],
            compiler_params=params(),
            name="encode",
        )(place, enc_scale, *pieces, small, shifted, kv_near, out_near)

    def windows(own, halo):
        return pl.pallas_call(
            window_kernel,
            out_shape=half_resid,
            in_specs=[SMEM, SMEM] + [VMEM] * 5,
            out_specs=VMEM,
            scratch_shapes=[
                pltpu.VMEM((WINDOWS * PADDED, 3 * D), bf16),
                pltpu.VMEM((WINDOWS * PADDED, 2 * D), bf16),
                pltpu.VMEM((WINDOWS * PADDED, D), bf16),
            ],
            compiler_params=params(),
            name="window",
        )(place, swin_scale, own, halo, small, qkv_near, proj_near)

    left = encode(0, near)
    from_right = move(left, 0, -1, lon_count)
    parts = along_y(after(held, left), lon_count)
    right = encode(1, lax.optimization_barrier((*near, left))[:4])
    from_left = move(after(right, from_right), 0, 1, lon_count)
    right_resid = windows(right, from_right)
    left_resid = windows(left, after(from_left, right_resid))
    mine = after(jnp.concatenate(parts, axis=0), from_left, right_resid)
    other = lax.ppermute(mine, "lat", [(a, a ^ 1) for a in range(4)])
    out_left, edges = pl.pallas_call(
        feed_first_kernel,
        out_shape=[half_block, struct((2 * EDGE, D), bf16)],
        in_specs=[VMEM] * 5,
        out_specs=[VMEM] * 2,
        compiler_params=params(),
        name="feed_first",
    )(left_resid, right_resid, small, near_by(mine), near_by(other))
    edges = move(edges, -1, 0, lon_count)
    out_right = pl.pallas_call(
        feed_rest_kernel,
        out_shape=struct((WINDOWS * PADDED - SKIP, D), bf16),
        in_specs=[VMEM] * 4,
        out_specs=VMEM,
        compiler_params=params(),
        name="feed_rest",
    )(after(right_resid, out_left), small, near_by(mine), near_by(other))
    joined = pl.pallas_call(
        join_kernel,
        out_shape=struct((LATENT, WW, ROWS, D), bf16),
        in_specs=[VMEM] * 3,
        out_specs=VMEM,
        scratch_shapes=[pltpu.VMEM((2, D // 128, WINDOWS * GROUP + 56, 128), f32)],
        compiler_params=params(),
        name="join",
    )(out_left, out_right, edges)
    return joined.transpose(0, 2, 1, 3)


def solution(mesh):
    return jax.shard_map(
        functools.partial(shards, mesh.shape["lon"]),
        mesh=mesh,
        in_specs=(
            P("lat", None, "lon"),
            P("lat", "lon"),
            P(),
            P(),
            P(),
            P(),
            P(),
            P(),
            P(),
            P(),
            P(),
            P(),
            P(),
            P(),
            P(),
            P(("lat", "lon"), None),
            P(("lat", "lon"), None),
        ),
        out_specs=P(None, "lat", "lon", None),
        check_vma=False,
    )
```

```python
import functools
import math

import jax
import jax.numpy as jnp
from jax import lax
from jax.experimental import pallas as pl
from jax.experimental.pallas import tpu as pltpu
from jax.sharding import PartitionSpec as P

WH = 6
WW = 12
HALF = WW // 2
SHIFT = WH // 2
LEVELS_EACH = 3
LATENT = 3
HEADS = 8
HEAD = 64
CHAN = 80
D = 512
ROWS = 24
SPAN = HALF * CHAN
WINDOWS = ROWS // WH
GROUP = WH * LATENT * HALF
PADDED = 112
STEP = LATENT * HALF
EDGE = 64
SKIP = 48
GAIN = 12
QUERY = 13
KIND = 16
ATTN = 19
MLP = 20

epsilon = 1e-05
masked_score = -1e30
f32 = jnp.float32
bf16 = jnp.bfloat16

VMEM = pl.BlockSpec(memory_space=pltpu.VMEM)
ANY = pl.BlockSpec(memory_space=pl.ANY)
SMEM = pl.BlockSpec(memory_space=pltpu.SMEM)


def dot(a, b):
    return jnp.dot(a, b, preferred_element_type=f32)


def dot_nt(a, b):
    return lax.dot_general(a, b, (((1,), (1,)), ((), ())), preferred_element_type=f32)


def layer_norm(values, gain_vector):
    average = jnp.mean(values, axis=-1, keepdims=True)
    centred = values - average
    spread = jnp.mean(centred * centred, axis=-1, keepdims=True)
    return centred * lax.rsqrt(spread + epsilon) * gain_vector


def pack_kernel(place, fields, kind, mlp_up, mlp_down, *rest):
    outs, held, staged = rest[:4], rest[4], rest[5]
    held[:, :D] = mlp_up[...]
    held[:, D:] = mlp_down[...]
    row_at = lax.broadcasted_iota(jnp.int32, (ROWS, ROWS), 0)
    col_at = lax.broadcasted_iota(jnp.int32, (ROWS, ROWS), 1)
    one_hot = jnp.where(row_at == col_at, 1.0, 0.0).astype(bf16)
    kinds = dot_nt(one_hot, kind[...].astype(f32).astype(bf16))
    kinds = jnp.concatenate([kinds[ROWS - SHIFT :], kinds[: ROWS - SHIFT]], axis=0)
    nothing = jnp.zeros((4, 3 * ROWS, D - SPAN), f32)
    staged[:, :, SPAN:D] = nothing
    staged[:, :, D + SPAN :] = nothing
    for level in range(LEVELS_EACH):
        part = fields[level].astype(f32)
        count = part.shape[0]
        part = jnp.concatenate([part[count - SHIFT :], part[: count - SHIFT]], axis=0)
        for to in range(4):
            rows = part[to * ROWS : (to + 1) * ROWS]
            at = slice(level * ROWS, (level + 1) * ROWS)
            staged[to, at, :SPAN] = rows[:, :SPAN]
            staged[to, at, D : D + SPAN] = rows[:, SPAN:]
    for to in range(4):
        staged[to, :ROWS, SPAN : SPAN + HALF] = kinds[:, :HALF]
        staged[to, :ROWS, D + SPAN : D + SPAN + HALF] = kinds[:, HALF:]
    for step in range(4):
        to = lax.rem(place[0] + step, 4)
        outs[step][...] = staged[to].astype(bf16)


def prepare_kernel(
    level_embed,
    enc_gain,
    latent_query,
    kind_embed,
    attn_gain,
    mlp_gain,
    patch_weight,
    *rest,
):
    fars, small, shifted, nears, sems = rest[:4], rest[4], rest[5], rest[6:10], rest[10]
    copies = [
        pltpu.make_async_copy(far, near, sems.at[at])
        for at, (far, near) in enumerate(zip(fars, nears))
    ]
    for copy in copies:
        copy.start()
    small[...] = jnp.concatenate(
        [
            level_embed[...],
            enc_gain[...],
            latent_query[...].astype(f32),
            kind_embed[...],
            attn_gain[...],
            mlp_gain[...],
            jnp.zeros((3, D), f32),
        ],
        axis=0,
    )
    shifted[...] = jnp.zeros(shifted.shape, bf16)
    for col in range(HALF):
        offset = col * CHAN % 128
        shifted[col, offset : offset + CHAN, :] = patch_weight[...]
    for copy in copies:
        copy.wait()


def encode_kernel(
    place,
    enc_scale,
    piece0,
    piece1,
    piece2,
    piece3,
    small,
    shifted,
    kv_weight,
    enc_out_weight,
    out,
    spread,
    *,
    side,
    chunk,
):
    lat = place[0]
    lanes = slice(side * D, (side + 1) * D)
    pieces = [piece[:, lanes].astype(f32) for piece in (piece0, piece1, piece2, piece3)]
    row_at = lax.broadcasted_iota(jnp.int32, (ROWS, D - SPAN), 0)
    kinds = jnp.where(row_at < SHIFT, pieces[1][:ROWS, SPAN:], pieces[0][:ROWS, SPAN:])
    patches = jnp.concatenate(pieces, axis=0).astype(bf16)
    embeds = []
    for step in range(4):
        start = lax.rem(lat - step + 4, 4) * LEVELS_EACH
        for level in range(LEVELS_EACH):
            embeds.append(
                jnp.broadcast_to(small[pl.ds(start + level, 1), :], (ROWS, D))
            )
    embeds = jnp.concatenate(embeds, axis=0)
    gain = small[GAIN : GAIN + 1]
    queries = small[QUERY : QUERY + LATENT]
    kind_embed = small[KIND : KIND + 3]
    head_at = lax.broadcasted_iota(jnp.int32, (HEADS, D), 0)
    lane_at = lax.broadcasted_iota(jnp.int32, (HEADS, D), 1) // HEAD
    in_head = jnp.where(head_at == lane_at, 1.0, 0.0).astype(f32)
    query_rows = jnp.concatenate(
        [in_head * queries[latent : latent + 1] for latent in range(LATENT)], axis=0
    ).astype(bf16)
    nothing = jnp.zeros((HEADS, D), f32)
    widen = [
        jnp.concatenate(
            [in_head if at == latent else nothing for at in range(LATENT)], axis=0
        ).astype(bf16)
        for latent in range(LATENT)
    ]
    lane = lax.broadcasted_iota(jnp.int32, (1, LATENT * HEADS), 1) % HEADS
    scale = jnp.zeros((1, LATENT * HEADS), f32)
    for head in range(HEADS):
        scale = jnp.where(lane == head, enc_scale[head] / math.sqrt(HEAD), scale)
    count = patches.shape[0]
    levels = count // ROWS
    for first in range(0, HALF, chunk):
        tokens = []
        for col in range(first, first + chunk):
            base = col * CHAN // 128 * 128
            depth = min(192, D - base)
            embedded = dot(patches[:, base : base + depth], shifted[col, :depth, :]) + embeds
            tokens.append(layer_norm(embedded, gain).astype(bf16))
        tokens = jnp.concatenate(tokens, axis=0)
        keys = dot(tokens, kv_weight[:, :D]).astype(bf16)
        values = dot(tokens, kv_weight[:, D:]).astype(bf16).astype(f32)
        scores = dot_nt(keys, query_rows) * scale
        scores = scores.reshape(chunk, levels, ROWS, LATENT * HEADS)
        highest = jnp.max(scores, axis=1, keepdims=True)
        raised = jnp.exp(scores - highest)
        weights = raised / jnp.sum(raised, axis=1, keepdims=True)
        weights = weights.reshape(chunk * count, LATENT * HEADS).astype(bf16)
        pooled = []
        for latent in range(LATENT):
            wide = dot(weights, widen[latent]) * values
            pooled.append(jnp.sum(wide.reshape(chunk, levels, ROWS, D), axis=1))
        pooled = jnp.concatenate(
            [pooled[latent][at] for at in range(chunk) for latent in range(LATENT)], axis=0
        ).astype(bf16)
        encoded = dot(pooled, enc_out_weight[...])
        for at in range(chunk):
            col = first + at
            kind = kinds[:, col : col + 1]
            kind_add = jnp.where(
                kind < 0.5,
                kind_embed[0:1],
                jnp.where(kind < 1.5, kind_embed[1:2], kind_embed[2:3]),
            )
            for latent in range(LATENT):
                start = (at * LATENT + latent) * ROWS
                value = encoded[start : start + ROWS] + queries[latent : latent + 1] + kind_add
                value = value.astype(bf16).astype(f32)
                for tile in range(D // 128):
                    spread[tile, pl.ds(latent * HALF + col, ROWS, stride=STEP), :] = value[
                        :, tile * 128 : (tile + 1) * 128
                    ]
    for tile in range(D // 128):
        spread[tile, WINDOWS * GROUP :, :] = jnp.zeros((8, 128), f32)
        for window in range(WINDOWS):
            out[window * PADDED : (window + 1) * PADDED, tile * 128 : (tile + 1) * 128] = spread[
                tile, pl.ds(window * GROUP, PADDED), :
            ].astype(bf16)


def window_kernel(
    place,
    swin_scale,
    own,
    halo,
    small,
    qkv_weight,
    proj_weight,
    resid,
    own_qkv,
    halo_kv,
    mixed,
):
    gain = small[ATTN : ATTN + 1]
    normed = layer_norm(own[...].astype(f32), gain).astype(bf16)
    own_qkv[...] = dot(normed, qkv_weight[...]).astype(bf16)
    normed = layer_norm(halo[...].astype(f32), gain).astype(bf16)
    halo_kv[...] = dot(normed, qkv_weight[:, D:]).astype(bf16)
    size = 2 * PADDED
    key_at = lax.broadcasted_iota(jnp.int32, (size, size), 1)
    key_at = jnp.where(key_at >= PADDED, key_at - PADDED, key_at)
    query_at = lax.broadcasted_iota(jnp.int32, (size, size), 0)
    query_at = jnp.where(query_at >= PADDED, query_at - PADDED, query_at)
    off = jnp.where(key_at < GROUP, 0.0, masked_score).astype(f32)
    apart = jnp.where((key_at < GROUP // 2) != (query_at < GROUP // 2), masked_score, 0.0)
    first_off = off + apart * jnp.where(place[0] == 0, 1.0, 0.0).astype(f32)
    off_row = off[0:1]
    lane = lax.broadcasted_iota(jnp.int32, (1, 128), 1)
    low = lane < HEAD
    sides = [jnp.where(low, 1.0, 0.0).astype(bf16), jnp.where(low, 0.0, 1.0).astype(bf16)]
    first_side = lax.broadcasted_iota(jnp.int32, (size, 1), 0) < PADDED
    unit = math.log2(math.e) / math.sqrt(HEAD)
    factors = [
        jnp.where(first_side, swin_scale[2 * pair] * unit, swin_scale[2 * pair + 1] * unit)
        for pair in range(HEADS // 2)
    ]
    for window in range(WINDOWS):
        rows = slice(window * PADDED, (window + 1) * PADDED)
        bias = first_off if window == 0 else off_row
        for pair in range(HEADS // 2):
            lanes = [slice(part * D + pair * 128, part * D + pair * 128 + 128) for part in range(3)]
            query = own_qkv[rows, lanes[0]]
            key = jnp.concatenate([own_qkv[rows, lanes[1]], halo_kv[rows, lanes[0]]], axis=0)
            value = jnp.concatenate([own_qkv[rows, lanes[2]], halo_kv[rows, lanes[1]]], axis=0)
            both = jnp.concatenate([query * sides[0], query * sides[1]], axis=0)
            scores = dot_nt(both, key) + bias
            highest = jnp.max(scores, axis=-1, keepdims=True)
            raised = jnp.exp2((scores - highest) * factors[pair])
            total = jnp.sum(raised, axis=-1, keepdims=True)
            weights = (raised * (1.0 / total)).astype(bf16)
            sums = dot(weights, value)
            mixed[rows, lanes[0]] = jnp.where(low, sums[:PADDED], sums[PADDED:]).astype(bf16)
    attended = dot(mixed[...], proj_weight[...]).astype(bf16).astype(f32)
    resid[...] = own[...].astype(f32) + attended


def feed_rows(values, gain, mine, other):
    tokens = layer_norm(values, gain).astype(bf16)
    total = values
    for block in (mine, other):
        for start in range(0, block.shape[0], 512):
            up = block[start : start + 512, :D]
            down = block[start : start + 512, D:]
            hidden = dot_nt(tokens, up)
            hidden = hidden * (1.0 + lax.erf(hidden * math.sqrt(0.5))) * 0.5
            total = total + dot(hidden.astype(bf16), down)
    return total.astype(bf16)


def feed_edges_kernel(left, right, small, mine, other, out):
    values = jnp.concatenate([left[:EDGE], right[:EDGE]], axis=0)
    out[...] = feed_rows(values, small[MLP : MLP + 1], mine, other)


def feed_rest_kernel(left, right, small, mine, other, out_left, out_right):
    values = jnp.concatenate([left[SKIP:], right[SKIP:]], axis=0)
    total = feed_rows(values, small[MLP : MLP + 1], mine, other)
    out_left[...] = total[: WINDOWS * PADDED - SKIP]
    out_right[...] = total[WINDOWS * PADDED - SKIP :]


def join_kernel(left, right, edges, out, held):
    for side, (source, skip) in enumerate(((left, SKIP), (right, SKIP))):
        for tile in range(D // 128):
            lanes = slice(tile * 128, (tile + 1) * 128)
            for window in range(WINDOWS):
                first = skip if window == 0 else 0
                start = window * PADDED - skip + first
                rows = source[start : start + PADDED - first, lanes].astype(f32)
                held[side, tile, window * GROUP + first : (window + 1) * GROUP, :] = rows[
                    : GROUP - first
                ]
            tail = edges[side * EDGE : (side + 1) * EDGE, lanes].astype(f32)
            held[side, tile, WINDOWS * GROUP :, :] = tail[:56]
        for latent in range(LATENT):
            for col in range(HALF):
                start = SHIFT * STEP + latent * HALF + col
                for tile in range(D // 128):
                    out[
                        latent, side * HALF + col, :, tile * 128 : (tile + 1) * 128
                    ] = held[side, tile, pl.ds(start, ROWS, stride=STEP), :].astype(bf16)


def params():
    return pltpu.CompilerParams(vmem_limit_bytes=32 * 1024 * 1024)


def struct(shape, dtype):
    return jax.ShapeDtypeStruct(shape, dtype)


def after(array, *others):
    return lax.optimization_barrier((array, *others))[0]


def along(held, bits, lon_count):
    unit = bits // 3
    moved = [
        lax.ppermute(
            held,
            "lon",
            [(i, (i & ~bits) | ((i + step * unit) & bits)) for i in range(lon_count)],
        )
        for step in (1, 2, 3)
    ]
    return jnp.concatenate([held] + moved, axis=0)


def along_y(held, lon_count):
    moved = [
        lax.ppermute(
            held,
            ("lat", "lon"),
            [
                (a * lon_count + b, ((a + 2 * far) % 4) * lon_count + (b ^ (16 * near)))
                for a in range(4)
                for b in range(lon_count)
            ],
        )
        for far, near in ((0, 1), (1, 0), (1, 1))
    ]
    return [held] + moved


def near_by(array):
    return pltpu.with_memory_space_constraint(array, pltpu.VMEM)


def far_off(array):
    return pltpu.with_memory_space_constraint(array, pltpu.HBM)


def move(array, lat_step, lon_step, lon_count):
    perm = [
        (a * lon_count + b, ((a + lat_step) % 4) * lon_count + (b + lon_step) % lon_count)
        for a in range(4)
        for b in range(lon_count)
    ]
    return lax.ppermute(array, ("lat", "lon"), perm)


def shards(
    lon_count,
    fields,
    surface_kind,
    patch_weight,
    level_embed,
    enc_gain,
    latent_query,
    kv_weight,
    enc_scale,
    enc_out_weight,
    kind_embed,
    attn_gain,
    qkv_weight,
    swin_scale,
    proj_weight,
    mlp_gain,
    mlp_up,
    mlp_down,
):
    place = lax.axis_index("lat").astype(jnp.int32).reshape(1)
    piece = struct((LEVELS_EACH * ROWS, 2 * D), bf16)
    *packed, held = pl.pallas_call(
        pack_kernel,
        out_shape=[piece] * 4 + [struct((mlp_up.shape[0], 2 * D), bf16)],
        in_specs=[SMEM] + [VMEM] * 4,
        out_specs=[VMEM] * 5,
        scratch_shapes=[pltpu.VMEM((4, LEVELS_EACH * ROWS, 2 * D), f32)],
        compiler_params=params(),
        name="pack",
    )(
        place,
        far_off(fields),
        far_off(surface_kind.T),
        far_off(mlp_up),
        far_off(mlp_down),
    )
    held = along(held, 3, lon_count)
    near = [packed[0]] + [move(packed[step], step, 0, lon_count) for step in (1, 2, 3)]
    held = along(held, 12, lon_count)
    half_block = struct((WINDOWS * PADDED, D), bf16)
    half_resid = struct((WINDOWS * PADDED, D), f32)

    weights = (kv_weight, enc_out_weight, qkv_weight, proj_weight)
    small, shifted, kv_near, out_near, qkv_near, proj_near = [
        near_by(array)
        for array in pl.pallas_call(
            prepare_kernel,
            out_shape=[pltpu.VMEM((24, D), f32), pltpu.VMEM((HALF, 192, D), bf16)]
            + [pltpu.VMEM(weight.shape, bf16) for weight in weights],
            in_specs=[VMEM] * 7 + [ANY] * 4,
            out_specs=[VMEM] * 6,
            scratch_shapes=[pltpu.SemaphoreType.DMA((4,))],
            compiler_params=params(),
            name="prepare",
        )(
            far_off(after(level_embed, *packed)),
            far_off(enc_gain.reshape(1, D)),
            far_off(latent_query),
            far_off(kind_embed),
            far_off(attn_gain.reshape(1, D)),
            far_off(mlp_gain.reshape(1, D)),
            far_off(patch_weight),
            *[far_off(weight) for weight in weights],
        )
    ]

    def encode(side, pieces):
        return pl.pallas_call(
            functools.partial(encode_kernel, side=side, chunk=6),
            out_shape=half_block,
            in_specs=[SMEM, SMEM] + [VMEM] * 8,
            out_specs=VMEM,
            scratch_shapes=[pltpu.VMEM((D // 128, WINDOWS * GROUP + 8, 128), f32)],
            compiler_params=params(),
            name="encode",
        )(place, enc_scale, *pieces, small, shifted, kv_near, out_near)

    def windows(own, halo):
        return pl.pallas_call(
            window_kernel,
            out_shape=half_resid,
            in_specs=[SMEM, SMEM] + [VMEM] * 5,
            out_specs=VMEM,
            scratch_shapes=[
                pltpu.VMEM((WINDOWS * PADDED, 3 * D), bf16),
                pltpu.VMEM((WINDOWS * PADDED, 2 * D), bf16),
                pltpu.VMEM((WINDOWS * PADDED, D), bf16),
            ],
            compiler_params=params(),
            name="window",
        )(place, swin_scale, own, halo, small, qkv_near, proj_near)

    left = encode(0, near)
    from_right = move(left, 0, -1, lon_count)
    parts = along_y(after(held, left), lon_count)
    right = encode(1, lax.optimization_barrier((*near, left))[:4])
    from_left = move(after(right, from_right), 0, 1, lon_count)
    right_resid = windows(right, from_right)
    left_resid = windows(left, after(from_left, right_resid))
    mine = after(jnp.concatenate(parts, axis=0), from_left, right_resid)
    other = lax.ppermute(mine, "lat", [(a, a ^ 1) for a in range(4)])
    feeds = (left_resid, right_resid, small, near_by(mine), near_by(other))
    edges = pl.pallas_call(
        feed_edges_kernel,
        out_shape=struct((2 * EDGE, D), bf16),
        in_specs=[VMEM] * 5,
        out_specs=VMEM,
        compiler_params=params(),
        name="feed_edges",
    )(*feeds)
    half_rest = struct((WINDOWS * PADDED - SKIP, D), bf16)
    out_left, out_right = pl.pallas_call(
        feed_rest_kernel,
        out_shape=[half_rest] * 2,
        in_specs=[VMEM] * 5,
        out_specs=[VMEM] * 2,
        compiler_params=params(),
        name="feed_rest",
    )(after(left_resid, edges), *feeds[1:])
    edges = move(edges, -1, 0, lon_count)
    joined = pl.pallas_call(
        join_kernel,
        out_shape=struct((LATENT, WW, ROWS, D), bf16),
        in_specs=[VMEM] * 3,
        out_specs=VMEM,
        scratch_shapes=[pltpu.VMEM((2, D // 128, WINDOWS * GROUP + 56, 128), f32)],
        compiler_params=params(),
        name="join",
    )(out_left, out_right, edges)
    return joined.transpose(0, 2, 1, 3)


def solution(mesh):
    return jax.shard_map(
        functools.partial(shards, mesh.shape["lon"]),
        mesh=mesh,
        in_specs=(
            P("lat", None, "lon"),
            P("lat", "lon"),
            P(),
            P(),
            P(),
            P(),
            P(),
            P(),
            P(),
            P(),
            P(),
            P(),
            P(),
            P(),
            P(),
            P(("lat", "lon"), None),
            P(("lat", "lon"), None),
        ),
        out_specs=P(None, "lat", "lon", None),
        check_vma=False,
    )
```
